256 devices in a mesh: section: 4 (over z_hi), tp: 64 (over z_lo, x, y, core).
Axes of the slice: x: 4, y: 4, z: 8 (z_hi: 4, z_lo: 2; z = z_hi * 2 + z_lo), core: 2. Of those that a mesh axis runs over, the one named last changes fastest.
Arguments:
- tokens: bfloat16 [4, 128, 8192], P('section', 'tp'), may hold values from -6 to 6
- norm_gain: bfloat16 [4, 8192], P('section'), may hold values from 0.5 to 1.5
- q_weight: bfloat16 [4, 8192, 8192], P('section', None, 'tp'), may hold values from -0.0625 to 0.0625
- q_bias: bfloat16 [4, 8192], P('section', 'tp'), may hold values from -8 to 8
- kv_weight: bfloat16 [4, 8192, 2048], P('section', 'tp'), may hold values from -0.0625 to 0.0625
- kv_bias: bfloat16 [4, 2048], P('section'), may hold values from -0.3125 to 0.3125
- out_weight: bfloat16 [4, 8192, 8192], P('section', 'tp'), may hold values from -5 to 5
- prefix_cache: bfloat16 [4, 16384, 2048], P('section', 'tp'), may hold values from -16 to 16
- span_lengths: int32 [4, 8], P('section'), may hold values from 1 to 32, 128 in all within a row
- prefix_lengths: int32 [4, 8], P('section'), may hold values from 1 to 4096, 16384 in all within a row
- slot_owner: int32 [4, 64], P('section'), may hold values from 0 to 63, each once within a row
- head_order: int32 [4, 8], P('section'), may hold values from 0 to 7, each once within a row
Outputs:
- handoff: bfloat16 [4, 128, 8192], P('section', 'tp')
- decode_kv: bfloat16 [4, 64, 32, 2048], P('section', 'tp')
The draws below stay inside these ranges and needn't reach their ends.
Inputs may be any that keep to these rules, and one draw needn't show every extreme that they name: `span_lengths`: 8 positive counts summing to 128; the largest is exactly 32. `prefix_lengths`: 8 positive counts summing to 16384; the largest is exactly 4096. `slot_owner`: each section's row is a permutation of the decode slots' numbers; entries below 8 name requests. `head_order`: each section's row is a permutation.
All inputs are finite; a program needn't handle non-finite values.
Results may differ from the reference program's by a relative error of at most 0.015.
Values may be sent and summed in bfloat16 or wider, within the bound.
No kernel may reach another device: no remote copies, remote signals or barrier semaphores. Data moves between devices by JAX's collectives and lax.ppermute only.
A program may use at most 128 MiB of HBM per device.

```python
import math
import jax
import jax.numpy as jnp
import numpy as np
from jax import lax

QH = 64
KVH = 8
HD = 128
D = 8192
SPAN = 128
REQS = 8
PREFIX = 16384
MOSTC = 32
PMOST = 4096
N_SECTION = 4
N_TP = 64


def draw_q_bias(key, part):
    key = jax.random.fold_in(key, 11)
    return (0.5 * jax.random.truncated_normal(key, -6.0, 6.0, (N_SECTION, QH * HD), jnp.float32)).astype(jnp.bfloat16)


def draw_prefix_cache(key, part):
    key = jax.random.fold_in(key, 12)
    full_shape = (N_SECTION, PREFIX, 2 * KVH * HD)
    return jax.random.truncated_normal(key, -6.0, 6.0, full_shape, jnp.float32).astype(jnp.bfloat16)


def shard_levels(own_key, dims, pieces, least, high):
    def one(axis_at, blocks):
        heights = jax.random.uniform(jax.random.fold_in(jax.random.fold_in(own_key, 6), axis_at), (blocks,), jnp.float32, least / len(pieces), high / len(pieces))
        return jnp.repeat(jnp.exp(heights), dims[axis_at] // blocks).reshape((-1,) + (1,) * (len(dims) - axis_at - 1))

    loudness = one(*pieces[0])
    for cut in pieces[1:]:
        loudness = loudness * one(*cut)
    return loudness


def profile(number_of, total, bound, slope):
    portions = [(1 << 20) // math.isqrt(grade ** slope) + 1 for grade in range(2, number_of + 1)]
    rest, holding = total - bound - (number_of - 1), [1] * (number_of - 1)
    while rest > 0:
        candidates = [i for i in range(number_of - 1) if holding[i] < bound]
        pool, remaining = sum([portions[i] for i in candidates]), rest
        for i in candidates:
            addition = min(bound - holding[i], max(1, remaining * portions[i] // pool), rest)
            holding[i] = holding[i] + addition
            rest = rest - addition
    return np.array([bound] + holding)


def ragged(stream_key, count, total, reach, lean):
    if count == 2:
        one = jax.random.randint(stream_key, (), max(1, total - reach), min(reach, total - 1) + 1)
        return jnp.stack([one, total - one])
    tallies = jnp.asarray(profile(count, total, reach, lean), jnp.int32)
    twos = (count - 1) // 2
    donor, receiver = tallies[1:1 + 2 * twos:2], tallies[2:2 + 2 * twos:2]
    slack = jnp.minimum(donor - 1, reach - receiver)
    passed = jax.random.randint(jax.random.fold_in(stream_key, 1), (twos,), 0, 1 << 20) % (slack + 1)
    tallies = tallies.at[1:1 + 2 * twos:2].set(donor - passed).at[2:2 + 2 * twos:2].set(receiver + passed)
    return tallies[jax.random.permutation(jax.random.fold_in(stream_key, 2), count)]


def gaussian(rng, extent, spread, most, cuts=(), held_as=jnp.bfloat16):
    result = spread * jax.random.normal(rng, extent, jnp.float32)
    if cuts:
        result = result * shard_levels(rng, extent, cuts, -0.22, 0.18)
    return jnp.clip(result, -most, most).astype(held_as)


def setup_inputs(seed: int = 0) -> dict:
    arg_keys = jax.random.split(jax.random.key(seed), 13)
    return {
        "tokens": gaussian(arg_keys[0], (N_SECTION, SPAN, D), 1.0, 6.0, ((0, 4), (1, 64))),
        "norm_gain": jnp.clip(1.0 + 0.1 * jax.random.normal(arg_keys[1], (N_SECTION, D), jnp.float32), 0.5, 1.5).astype(jnp.bfloat16),
        "q_weight": gaussian(arg_keys[2], (N_SECTION, D, QH * HD), D ** -0.5, 0.0625, ((0, 4), (2, 64))),
        "q_bias": draw_q_bias(jax.random.fold_in(arg_keys[12], 71), 0),
        "kv_weight": gaussian(arg_keys[4], (N_SECTION, D, 2 * KVH * HD), D ** -0.5, 0.0625, ((0, 4), (1, 64))),
        "kv_bias": gaussian(arg_keys[5], (N_SECTION, 2 * KVH * HD), 0.02, 0.3125, ((0, 4),)),
        "out_weight": gaussian(arg_keys[6], (N_SECTION, QH * HD, D), 0.37, 5.0, ((0, 4), (1, 64))),
        "prefix_cache": draw_prefix_cache(jax.random.fold_in(arg_keys[12], 71), 0),
        "span_lengths": jax.vmap(lambda own: ragged(own, REQS, SPAN, MOSTC, 2))(jax.random.split(arg_keys[8], N_SECTION)).reshape((N_SECTION, REQS)).astype(jnp.int32),
        "prefix_lengths": jax.vmap(lambda own: ragged(own, REQS, PREFIX, PMOST, 2))(jax.random.split(arg_keys[9], N_SECTION)).reshape((N_SECTION, REQS)).astype(jnp.int32),
        "slot_owner": jax.vmap(lambda own: jax.random.permutation(own, N_TP))(jax.random.split(arg_keys[10], N_SECTION)).reshape((N_SECTION, N_TP)).astype(jnp.int32),
        "head_order": jax.vmap(lambda own: jax.random.permutation(own, KVH))(jax.random.split(arg_keys[11], N_SECTION)).reshape((N_SECTION, KVH)).astype(jnp.int32),
    }


epsilon = 1e-06
masked_score = -1e+30

def segment_of(positions, lengths):
    ends = jnp.cumsum(lengths).astype(jnp.int32)
    return lax.optimization_barrier(jnp.sum((positions[:, None] >= ends[None, :]).astype(jnp.int32), axis=1)).astype(jnp.int32)

def norm_rows(tokens, gain):
    values = tokens.astype(jnp.float32)
    mean_square = lax.optimization_barrier(jnp.mean(values * values, axis=-1, keepdims=True))
    return (values * lax.rsqrt(mean_square + epsilon) * gain.astype(jnp.float32)).astype(jnp.bfloat16)

def one_section(tokens, gain, q_weight, q_bias, kv_weight, kv_bias, out_weight, cache, span_len, prefix_len, owners, order):
    group_size = QH // KVH
    score_scale = HD ** (-0.5)
    normed = norm_rows(tokens, gain)
    queries = (jnp.dot(normed, q_weight, preferred_element_type=jnp.float32) + q_bias.astype(jnp.float32)).astype(jnp.bfloat16)
    new_kv = (jnp.dot(normed, kv_weight, preferred_element_type=jnp.float32) + kv_bias.astype(jnp.float32)).astype(jnp.bfloat16)
    key_rows = jnp.concatenate([cache, new_kv], axis=0)
    span_pos = jnp.arange(SPAN, dtype=jnp.int32)
    query_seg = segment_of(span_pos, span_len)
    key_seg = jnp.concatenate([segment_of(jnp.arange(PREFIX, dtype=jnp.int32), prefix_len), query_seg])
    key_pos = jnp.concatenate([jnp.full((PREFIX,), -1, jnp.int32), span_pos])
    allowed = (key_seg[None, :] == query_seg[:, None]) & (key_pos[None, :] <= span_pos[:, None])
    grouped = queries.reshape(SPAN, KVH, group_size, HD)

    def per_head(kv_head):
        query_block = lax.dynamic_index_in_dim(grouped, kv_head, 1, keepdims=False).astype(jnp.float32)
        key_block = lax.dynamic_slice_in_dim(key_rows, kv_head * HD, HD, 1).astype(jnp.float32)
        value_block = lax.dynamic_slice_in_dim(key_rows, (KVH + kv_head) * HD, HD, 1).astype(jnp.float32)
        scores = jnp.einsum('cgh,kh->cgk', query_block, key_block) * score_scale
        scores = jnp.where(allowed[:, None, :], scores, masked_score)
        row_max = lax.optimization_barrier(jnp.max(scores, axis=2, keepdims=True))
        weights = lax.optimization_barrier(jnp.exp(scores - row_max).astype(jnp.bfloat16)).astype(jnp.float32)
        totals = lax.optimization_barrier(jnp.sum(weights, axis=2))
        value_sums = jnp.einsum('cgk,kh->cgh', weights, value_block)
        return value_sums / totals[:, :, None]
    heads_out = lax.map(per_head, jnp.arange(KVH, dtype=jnp.int32))
    attended = jnp.transpose(heads_out, (1, 0, 2, 3)).reshape(SPAN, QH * HD).astype(jnp.bfloat16)
    mixed = (tokens.astype(jnp.float32) + jnp.dot(attended, out_weight, preferred_element_type=jnp.float32)).astype(jnp.bfloat16)
    starts = (jnp.cumsum(span_len) - span_len).astype(jnp.int32)
    live = owners < REQS
    request = jnp.minimum(owners, REQS - 1)
    offsets = jnp.arange(MOSTC, dtype=jnp.int32)
    row_index = jnp.clip(starts[request][:, None] + offsets[None, :], 0, SPAN - 1)
    valid = live[:, None] & (offsets[None, :] < span_len[request][:, None])
    picked = jnp.take(new_kv, row_index, axis=0)
    picked = jnp.where(valid[:, :, None], picked, jnp.zeros_like(picked))
    reordered = jnp.take(picked.reshape(N_TP, MOSTC, 2, KVH, HD), order, axis=3)
    return (mixed, reordered.reshape(N_TP, MOSTC, 2 * KVH * HD))

def reference(tokens, norm_gain, q_weight, q_bias, kv_weight, kv_bias, out_weight, prefix_cache, span_lengths, prefix_lengths, slot_owner, head_order):
    mixed_all = []
    decode_all = []
    for section_id in range(N_SECTION):
        mixed, decode = one_section(tokens[section_id], norm_gain[section_id], q_weight[section_id], q_bias[section_id], kv_weight[section_id], kv_bias[section_id], out_weight[section_id], prefix_cache[section_id], span_lengths[section_id], prefix_lengths[section_id], slot_owner[section_id], head_order[section_id])
        mixed_all.append(mixed)
        decode_all.append(decode)
    handoff = jnp.roll(jnp.stack(mixed_all), 1, axis=0)
    return (handoff, jnp.stack(decode_all))
```

```python
import jax
import jax.numpy as jnp
from jax import lax
from jax.experimental import pallas as pl
from jax.experimental.pallas import tpu as pltpu
from jax.sharding import Mesh, PartitionSpec as P

QH = 64
KVH = 8
HD = 128
D = 8192
SPAN = 128
REQS = 8
MOSTC = 32
ROWS = 256
EPS = 1e-06
NEG = -1e30
SCALE = HD ** (-0.5)
SIZES = {"section": 4, "zl": 2, "x": 4, "y": 4, "core": 2}
TP = ("zl", "x", "y", "core")
F32 = jnp.float32
BF16 = jnp.bfloat16
VMEM = pl.BlockSpec(memory_space=pltpu.VMEM)
SMEM = pl.BlockSpec(memory_space=pltpu.SMEM)


def dot(a, b, ca, cb):
    return lax.dot_general(a, b, (((ca,), (cb,)), ((), ())), preferred_element_type=F32)


def swap_core(block):
    return lax.ppermute(block, "core", [(0, 1), (1, 0)])


def shift(block, axis, by):
    n = SIZES[axis]
    return lax.ppermute(block, axis, [(i, (i + by) % n) for i in range(n)])


def project_kernel(sc, own, other, gain, qw, kvt, qb, kvb, out):
    blk = 1024

    def step(i, carry):
        ss, aq, akv = carry
        at = pl.multiple_of(i * blk, blk)
        cols = pl.ds(at, blk)
        x = jnp.concatenate([own[:, cols], other[:, cols]], axis=0).astype(F32)
        ss = ss + jnp.sum(x * x, axis=1, keepdims=True)
        y = (x * gain[:, cols].astype(F32)).astype(BF16)
        aq = aq + dot(y, qw[cols, :], 1, 0)
        akv = akv + dot(y, kvt[:, cols], 1, 1)
        return ss, aq, akv

    zero = (jnp.zeros((SPAN, 1), F32), jnp.zeros((SPAN, HD), F32), jnp.zeros((SPAN, 32), F32))
    ss, aq, akv = lax.fori_loop(0, D // blk, step, zero, unroll=True)
    rs = lax.rsqrt(ss * (1.0 / D) + EPS)
    q = (aq * rs + qb[...].astype(F32)).astype(BF16)
    kv = (akv * rs + kvb[...].astype(F32)).astype(BF16)
    row = lax.broadcasted_iota(jnp.int32, (SPAN, SPAN), 0)
    col = lax.broadcasted_iota(jnp.int32, (SPAN, SPAN), 1)
    inner = row % 64
    core = jnp.where(row < 64, sc[0], 1 - sc[0])
    natural = (inner // 2) * 4 + core * 2 + inner % 2
    place = jnp.where(natural == col, 1.0, 0.0).astype(BF16)
    out[0:HD, :] = dot(q, place, 0, 0).astype(BF16)
    out[HD:HD + 32, :] = dot(kv, place, 0, 0).astype(BF16)


def attend_kernel(sc, span_len, prefix_len, mine, theirs, cache, part_mine, part_theirs, fresh, ktn, vtn):
    core, y, j = sc[0], sc[1], sc[2]
    blocks = []
    for ref, flip in ((mine, False), (theirs, True)):
        for k in range(4):
            src_core = 1 - core if flip else core
            src = ((y - k + 4) % 4) * 2 + src_core
            at = pl.multiple_of(src * 16, 16)
            ktn[pl.ds(at, 16), :] = ref[k, HD:HD + 16, :]
            vtn[pl.ds(at, 16), :] = ref[k, HD + 16:HD + 32, :]
            blocks.append(ref[k, 0:HD, :])
    qt = jnp.concatenate(blocks, axis=1)
    fresh[0:HD, :] = ktn[...]
    fresh[HD:2 * HD, :] = vtn[...]

    tok = lax.broadcasted_iota(jnp.int32, (1, SPAN), 1)
    key_tok = lax.broadcasted_iota(jnp.int32, (SPAN, 1), 0)
    q_seg = jnp.zeros((1, SPAN), jnp.int32)
    k_seg = jnp.zeros((SPAN, 1), jnp.int32)
    end = jnp.int32(0)
    for r in range(REQS):
        end = end + span_len[r]
        q_seg = q_seg + (tok >= end).astype(jnp.int32)
        k_seg = k_seg + (key_tok >= end).astype(jnp.int32)
    ends = []
    end = jnp.int32(0)
    for r in range(REQS):
        end = end + prefix_len[r]
        ends.append(end)

    def masked(s, allowed):
        parts = [
            jnp.where(allowed, s[:, u * SPAN:(u + 1) * SPAN], NEG) for u in range(KVH)
        ]
        return jnp.concatenate(parts, axis=1)

    allowed = (k_seg == q_seg) & (key_tok <= tok) & (key_tok // 16 == j)
    s = masked(dot(ktn[...], qt, 0, 0) * SCALE, allowed)
    m = jnp.max(s, axis=0, keepdims=True)
    p = jnp.exp(s - m)
    l = jnp.sum(p, axis=0, keepdims=True)
    o = dot(vtn[...], p.astype(BF16), 1, 0)

    for i in range(8):
        pos = (i * 8 + j) * ROWS + lax.broadcasted_iota(jnp.int32, (ROWS, 1), 0)
        seg = jnp.zeros((ROWS, 1), jnp.int32)
        for r in range(REQS):
            seg = seg + (pos >= ends[r]).astype(jnp.int32)
        s = masked(dot(cache[i, 0], qt, 1, 0) * SCALE, seg == q_seg)
        m_new = jnp.maximum(m, jnp.max(s, axis=0, keepdims=True))
        p = jnp.exp(s - m_new)
        alpha = jnp.exp(m - m_new)
        l = l * alpha + jnp.sum(p, axis=0, keepdims=True)
        o = o * alpha + dot(cache[i, 1], p.astype(BF16), 0, 0)
        m = m_new

    some = m > 0.5 * NEG
    inv = jnp.where(some, 1.0 / l, 0.0)
    lse = jnp.where(some, m + jnp.log(l), NEG)
    o = (o * inv).astype(BF16)
    hi = lse.astype(BF16)
    rest = lse - hi.astype(F32)
    mid = rest.astype(BF16)
    low = (rest - mid.astype(F32)).astype(BF16)
    at_row = lax.broadcasted_iota(jnp.int32, (16, SPAN), 0)
    for u in range(8):
        ref, k = (part_mine, u) if u < 4 else (part_theirs, u - 4)
        cols = slice(u * SPAN, (u + 1) * SPAN)
        ref[k, 0:HD, :] = o[:, cols]
        stats = jnp.where(
            at_row == 0,
            hi[:, cols].astype(F32),
            jnp.where(at_row == 1, mid[:, cols].astype(F32), low[:, cols].astype(F32)),
        )
        ref[k, HD:HD + 16, :] = stats.astype(BF16)


def merge_kernel(a, b, c, d, out):
    pieces = [(ref, i) for ref in (a, b, c, d) for i in range(2)]
    lse = []
    for ref, i in pieces:
        stats = ref[i, HD:HD + 16, :].astype(F32)
        lse.append(stats[0:1, :] + stats[1:2, :] + stats[2:3, :])
    top = lse[0]
    for one in lse[1:]:
        top = jnp.maximum(top, one)
    total = jnp.zeros((1, SPAN), F32)
    acc = jnp.zeros((HD, SPAN), F32)
    for (ref, i), one in zip(pieces, lse):
        w = jnp.exp(one - top)
        total = total + w
        acc = acc + ref[i, 0:HD, :].astype(F32) * w
    out[...] = (acc / total).astype(BF16)


def decode_kernel(sc, span_len, order, fresh, out):
    owner = sc[3]
    start = jnp.int32(0)
    count = jnp.int32(0)
    for r in range(REQS):
        start = start + jnp.where(r < owner, span_len[r], 0)
        count = count + jnp.where(r == owner, span_len[r], 0)
    row = lax.broadcasted_iota(jnp.int32, (MOSTC, SPAN), 0)
    col = lax.broadcasted_iota(jnp.int32, (MOSTC, SPAN), 1)
    pick = jnp.where((row < count) & (col == start + row), 1.0, 0.0).astype(BF16)
    for p in range(KVH):
        both = dot(pick, fresh[order[p]], 1, 1).astype(BF16)
        out[:, p * HD:(p + 1) * HD] = both[:, :HD]
        out[:, (KVH + p) * HD:(KVH + p + 1) * HD] = both[:, HD:]


def call(kernel, out_shape, n_smem, n_vmem, scratch=(), flops=1000000, data=1000000):
    many = isinstance(out_shape, tuple)
    return pl.pallas_call(
        kernel,
        out_shape=out_shape,
        in_specs=[SMEM] * n_smem + [VMEM] * n_vmem,
        out_specs=tuple(VMEM for _ in out_shape) if many else VMEM,
        scratch_shapes=list(scratch),
        compiler_params=pltpu.CompilerParams(vmem_limit_bytes=48 * 1024 * 1024),
        cost_estimate=pl.CostEstimate(flops=flops, bytes_accessed=data, transcendentals=0),
    )


def on_device(
    tokens,
    norm_gain,
    q_weight,
    q_bias,
    kv_weight,
    kv_bias,
    out_weight,
    prefix_cache,
    span_lengths,
    prefix_lengths,
    slot_owner,
    head_order,
):
    core = lax.axis_index("core")
    y = lax.axis_index("y")
    j = y * 2 + core
    g = lax.axis_index(("zl", "x"))
    me = g * 8 + j
    half = D // 2
    span_len = span_lengths[0]
    owner = lax.dynamic_index_in_dim(slot_owner[0], me, 0, keepdims=False)
    sc = jnp.stack([core, y, j, owner]).astype(jnp.int32)

    own = lax.all_to_all(
        jnp.broadcast_to(tokens, (32, 2, D)), ("zl", "x", "y"), 0, 0, tiled=True
    ).reshape(64, D)
    other = swap_core(own)

    kvt = kv_weight[0].T.reshape(2, KVH, 8, 16, HD).transpose(1, 2, 0, 3, 4).reshape(64, 32, HD)
    kvt = lax.all_to_all(kvt, TP, 0, 0, tiled=True)
    kvt = kvt.transpose(1, 0, 2).reshape(32, D)
    kvb = lax.dynamic_slice(kv_bias[0].reshape(2, 64, 16), (0, me, 0), (2, 1, 16)).reshape(1, 32)

    cache = prefix_cache[0].reshape(ROWS, 2, KVH, HD).transpose(2, 1, 0, 3)
    cache = lax.all_to_all(cache, ("zl", "x"), 0, 0, tiled=True)

    ow = out_weight[0]
    ow_mine = lax.dynamic_slice_in_dim(ow, core * half, half, 1)
    ow_theirs = swap_core(lax.dynamic_slice_in_dim(ow, (1 - core) * half, half, 1))
    tok_mine = lax.dynamic_slice_in_dim(tokens[0], core * half, half, 1)
    tok_theirs = swap_core(lax.dynamic_slice_in_dim(tokens[0], (1 - core) * half, half, 1))

    piece = call(
        project_kernel, jax.ShapeDtypeStruct((HD + 32, SPAN), BF16), 1, 7,
        flops=2 * SPAN * D * 256, data=5 << 20,
    )(sc, own, other, norm_gain, q_weight[0], kvt, q_bias, kvb)

    mine = jnp.stack([piece] + [shift(piece, "y", k) for k in range(1, 4)])
    theirs = swap_core(mine)

    part = jax.ShapeDtypeStruct((4, HD + 16, SPAN), BF16)
    part_mine, part_theirs, fresh = call(
        attend_kernel,
        (part, part, jax.ShapeDtypeStruct((2 * HD, SPAN), BF16)),
        3, 3,
        scratch=(pltpu.VMEM((HD, SPAN), BF16), pltpu.VMEM((HD, SPAN), BF16)),
        flops=4 * 1024 * 2048 * 128, data=20 << 20,
    )(sc, span_len, prefix_lengths[0], mine, theirs, cache)

    swapped = swap_core(part_theirs)
    pairs = [jnp.stack([part_mine[k], swapped[k]]) for k in range(4)]
    pairs = [pairs[0]] + [shift(pairs[k], "y", -k) for k in range(1, 4)]
    att = call(merge_kernel, jax.ShapeDtypeStruct((HD, SPAN), BF16), 0, 4)(*pairs)

    att_other = swap_core(att)
    mixed = dot(
        jnp.concatenate([att, att_other], axis=0),
        jnp.concatenate([ow_mine, ow_theirs], axis=0),
        0,
        0,
    ).astype(BF16)
    mixed = lax.all_to_all(mixed.reshape(32, 4, half), ("zl", "x", "y"), 0, 0, tiled=True)
    total = jnp.sum(mixed.astype(F32), axis=0).reshape(2, 2, half)
    same = lax.dynamic_index_in_dim(total, core, 0, keepdims=False)
    cross = lax.dynamic_index_in_dim(total, 1 - core, 0, keepdims=False)
    same = (same + tok_mine.astype(F32)).astype(BF16)
    cross = (cross + tok_theirs.astype(F32)).astype(BF16)
    n = SIZES["section"]
    route = [(s * 2 + c, ((s + 1) % n) * 2 + c) for s in range(n) for c in range(2)]
    same = lax.ppermute(same, ("section", "core"), route)
    route = [(s * 2 + c, ((s + 1) % n) * 2 + 1 - c) for s in range(n) for c in range(2)]
    cross = lax.ppermute(cross, ("section", "core"), route)
    handoff = jnp.where(
        core == 0,
        jnp.concatenate([same, cross], axis=1),
        jnp.concatenate([cross, same], axis=1),
    )

    every = lax.all_to_all(
        jnp.broadcast_to(fresh[None], (8, 2 * HD, SPAN)), ("zl", "x"), 0, 0, tiled=True
    )
    decode = call(decode_kernel, jax.ShapeDtypeStruct((MOSTC, 2 * KVH * HD), BF16), 3, 1)(
        sc, span_len, head_order[0], every
    )
    return (handoff[None], decode[None, None])


def solution(mesh):
    fine = Mesh(mesh.devices.reshape(4, 2, 4, 4, 2), tuple(SIZES))
    placed = (
        P("section", TP, None),
        P("section", None),
        P("section", None, TP),
        P("section", TP),
        P("section", TP, None),
        P("section", None),
        P("section", TP, None),
        P("section", TP, None),
        P("section", None),
        P("section", None),
        P("section", None),
        P("section", None),
    )
    return jax.shard_map(
        on_device,
        mesh=fine,
        in_specs=placed,
        out_specs=(P("section", TP, None), P("section", TP, None, None)),
        check_vma=False,
    )
```

```python
import jax
import jax.numpy as jnp
from jax import lax
from jax.experimental import pallas as pl
from jax.experimental.pallas import tpu as pltpu
from jax.sharding import Mesh, PartitionSpec as P

QH = 64
KVH = 8
HD = 128
D = 8192
SPAN = 128
REQS = 8
MOSTC = 32
ROWS = 256
EPS = 1e-06
NEG = -1e30
SCALE = HD ** (-0.5)
SIZES = {"section": 4, "zl": 2, "x": 4, "y": 4, "core": 2}
TP = ("zl", "x", "y", "core")
F32 = jnp.float32
BF16 = jnp.bfloat16
VMEM = pl.BlockSpec(memory_space=pltpu.VMEM)
SMEM = pl.BlockSpec(memory_space=pltpu.SMEM)


def dot(a, b, ca, cb):
    return lax.dot_general(a, b, (((ca,), (cb,)), ((), ())), preferred_element_type=F32)


def swap_core(block):
    return lax.ppermute(block, "core", [(0, 1), (1, 0)])


def flip_x(block, by):
    return lax.ppermute(block, "x", [(i, i ^ by) for i in range(4)])


def shift(block, axis, by):
    n = SIZES[axis]
    return lax.ppermute(block, axis, [(i, (i + by) % n) for i in range(n)])


def token_at(place):
    return ((place % 64) // 2) * 4 + (place // 64) * 2 + place % 2


def gathered_order(sc):
    row = lax.broadcasted_iota(jnp.int32, (SPAN, SPAN), 0)
    col = lax.broadcasted_iota(jnp.int32, (SPAN, SPAN), 1)
    core = jnp.where(row < 64, sc[0], 1 - sc[0])
    inner = row % 64
    y = (sc[1] - inner // 16 + 4) % 4
    place = core * 64 + (((inner % 16) // 2) * 4 + y) * 2 + inner % 2
    return jnp.where(place == col, 1.0, 0.0).astype(BF16)


def spread_kernel(tokens, out):
    one = tokens[...]
    for p in range(8):
        out[p] = one


def cut_kernel(cache, mine, theirs, out):
    for g in range(8):
        cols = slice(g * HD, (g + 1) * HD)
        out[g, :, 0:HD] = cache[:, cols]
        out[g, :, HD:2 * HD] = cache[:, (KVH + g) * HD:(KVH + g + 1) * HD]
        out[g, 0:HD, 2 * HD:] = mine[:, cols]
        out[g, HD:, 2 * HD:] = theirs[:, cols]


def project_kernel(sc, gain, qw, qb, bias, blocks, *rest):
    tokens, out = rest[:8], rest[8]
    core, y = sc[0], sc[1]
    blk = 1024
    ss = jnp.zeros((SPAN, 1), F32)
    aq = jnp.zeros((SPAN, HD), F32)
    for i in range(D // blk):
        cols = slice(i * blk, (i + 1) * blk)
        x = jnp.concatenate([ref[:, cols] for ref in tokens], axis=0).astype(F32)
        ss = ss + jnp.sum(x * x, axis=1, keepdims=True)
        h = (x * gain[:, cols].astype(F32)).astype(BF16)
        aq = aq + dot(h, qw[cols, :], 1, 0)
    akv = jnp.zeros((SPAN, HD), F32)
    for g in range(8):
        parts = []
        for owner in (core, 1 - core):
            cols = pl.ds(pl.multiple_of(((g * 4 + y) * 2 + owner) * HD, HD), HD)
            x = jnp.concatenate([ref[:, cols] for ref in tokens], axis=0).astype(F32)
            parts.append((x * gain[:, cols].astype(F32)).astype(BF16))
        akv = akv + dot(jnp.concatenate(parts, axis=1), blocks[g, :, 2 * HD:], 1, 0)
    rs = lax.rsqrt(ss * (1.0 / D) + EPS)
    q = ((aq * rs + qb[...].astype(F32)) * SCALE).astype(BF16)
    kv = (akv * rs + jnp.where(y == 0, 1.0, 0.0) * bias[...].astype(F32)).astype(BF16)
    out[...] = dot(jnp.concatenate([q, kv], axis=1), gathered_order(sc), 0, 0).astype(BF16)


def pack_kernel(a, b, c, d, out, fresh):
    total = jnp.zeros((HD, SPAN), F32)
    for k, ref in enumerate((a, b, c, d)):
        out[k * HD:(k + 1) * HD, :] = ref[0:HD, :]
        total = total + ref[HD:, :].astype(F32)
    rows = total.astype(BF16)
    out[4 * HD:, :] = rows
    fresh[...] = rows


def attend_kernel(sc, span_len, prefix_len, mine, theirs, blocks, part_mine, part_theirs):
    core, j = sc[0], sc[2]
    packs = (mine, theirs)
    qt = jnp.concatenate([ref[k * HD:(k + 1) * HD, :] for ref in packs for k in range(4)], axis=1)
    fresh = [ref[4 * HD:, :].astype(F32) for ref in packs]
    keys = jnp.where(core == 0, fresh[0], fresh[1]).astype(BF16)
    values = jnp.where(core == 0, fresh[1], fresh[0]).astype(BF16)

    tok = token_at(lax.broadcasted_iota(jnp.int32, (1, SPAN), 1))
    key_tok = token_at(lax.broadcasted_iota(jnp.int32, (SPAN, 1), 0))
    q_seg = jnp.zeros((1, SPAN), jnp.int32)
    k_seg = jnp.zeros((SPAN, 1), jnp.int32)
    end = jnp.int32(0)
    for r in range(REQS):
        end = end + span_len[r]
        q_seg = q_seg + (tok >= end).astype(jnp.int32)
        k_seg = k_seg + (key_tok >= end).astype(jnp.int32)
    ends = []
    end = jnp.int32(0)
    for r in range(REQS):
        end = end + prefix_len[r]
        ends.append(end)

    def masked(s, allowed):
        parts = [jnp.where(allowed, s[:, u * SPAN:(u + 1) * SPAN], NEG) for u in range(KVH)]
        return jnp.concatenate(parts, axis=1)

    allowed = (k_seg == q_seg) & (key_tok <= tok) & (key_tok // 16 == j)
    s = masked(dot(keys, qt, 0, 0), allowed)
    m = jnp.max(s, axis=0, keepdims=True)
    p = jnp.exp(s - m)
    l = jnp.sum(p, axis=0, keepdims=True)
    o = dot(values, p.astype(BF16), 1, 0)

    for i in range(8):
        first = (i * 8 + j) * ROWS
        pos = first + lax.broadcasted_iota(jnp.int32, (ROWS, 1), 0)
        seg = jnp.zeros((ROWS, 1), jnp.int32)
        for r in range(REQS):
            seg = seg + (pos >= ends[r]).astype(jnp.int32)
        s = masked(dot(blocks[i, :, 0:HD], qt, 1, 0), seg == q_seg)
        m_new = jnp.maximum(m, jnp.max(s, axis=0, keepdims=True))
        p = jnp.exp(s - m_new)
        alpha = jnp.exp(m - m_new)
        l = l * alpha + jnp.sum(p, axis=0, keepdims=True)
        o = o * alpha + dot(blocks[i, :, HD:2 * HD], p.astype(BF16), 0, 0)
        m = m_new

    some = m > 0.5 * NEG
    o = o * jnp.where(some, 1.0 / l, 0.0)
    lse = jnp.where(some, m + jnp.log(l), NEG)
    first = core == 0

    def by_token_core(row, k):
        a, b = row[:, k * SPAN:(k + 1) * SPAN], row[:, (4 + k) * SPAN:(5 + k) * SPAN]
        a, b = jnp.where(first, a, b), jnp.where(first, b, a)
        low = jnp.concatenate([a[:, :64], b[:, :64]], axis=1)
        high = jnp.concatenate([a[:, 64:], b[:, 64:]], axis=1)
        return jnp.where(first, low, high), jnp.where(first, high, low)

    at_row = lax.broadcasted_iota(jnp.int32, (16, SPAN), 0)
    for k in range(4):
        for ref, value, one in zip((part_mine, part_theirs), by_token_core(o, k), by_token_core(lse, k)):
            hi = one.astype(BF16).astype(F32)
            mid = (one - hi).astype(BF16).astype(F32)
            stats = jnp.where(at_row == 0, hi, jnp.where(at_row == 1, mid, one - hi - mid))
            ref[k, 0:HD, :] = value.astype(BF16)
            ref[k, HD:HD + 16, :] = stats.astype(BF16)


def mix_kernel(sc, a, b, c, d, ow_mine, ow_theirs, out, here, sems):
    blk = 1024
    copies = []
    for i in range(D // blk):
        cols = pl.ds(i * blk, blk)
        for h, ref in enumerate((ow_mine, ow_theirs)):
            to = here.at[pl.ds(h * HD, HD), cols]
            copies.append(pltpu.make_async_copy(ref.at[:, cols], to, sems.at[2 * i + h]))
            copies[-1].start()
    pieces = [(ref, i) for ref in (a, b, c, d) for i in range(2)]
    lse = []
    for ref, i in pieces:
        stats = ref[i, HD:HD + 16, :].astype(F32)
        lse.append(stats[0:1, :] + stats[1:2, :] + stats[2:3, :])
    top = lse[0]
    for one in lse[1:]:
        top = jnp.maximum(top, one)
    total = jnp.zeros((1, SPAN), F32)
    acc = jnp.zeros((HD, SPAN), F32)
    for (ref, i), one in zip(pieces, lse):
        w = jnp.exp(one - top)
        total = total + w
        acc = acc + ref[i, 0:HD, :].astype(F32) * w
    att = jnp.transpose(acc / total)
    first = sc[0] == 0
    mine = jnp.where(first, att[:64], att[64:])
    theirs = jnp.where(first, att[64:], att[:64])
    rows = jnp.concatenate([mine, theirs], axis=1).astype(BF16)
    for i in range(D // blk):
        cols = slice(i * blk, (i + 1) * blk)
        copies[2 * i].wait()
        copies[2 * i + 1].wait()
        sums = dot(rows, here[:, cols], 1, 0)
        for p in range(32):
            out[p, :, cols] = sums[2 * p:2 * p + 2].astype(BF16)


def decode_kernel(sc, span_len, order, other_owner, near, away, mine, theirs):
    zl, x = sc[4], sc[5]
    row = lax.broadcasted_iota(jnp.int32, (MOSTC, SPAN), 0)
    col = lax.broadcasted_iota(jnp.int32, (MOSTC, SPAN), 1)
    picks = []
    for owner in (sc[3], other_owner[0]):
        start = jnp.int32(0)
        count = jnp.int32(0)
        for r in range(REQS):
            start = start + jnp.where(r < owner, span_len[r], 0)
            count = count + jnp.where(r == owner, span_len[r], 0)
        picks.append(jnp.where((row < count) & (token_at(col) == start + row), 1.0, 0.0).astype(BF16))
    pick = jnp.concatenate(picks, axis=0)
    for far, ref in enumerate((near, away)):
        for k in range(4):
            head = ((zl + far) % 2) * 4 + (x ^ k)
            place = jnp.int32(0)
            for p in range(KVH):
                place = place + jnp.where(order[p] == head, p, 0)
            both = dot(pick, ref[k], 1, 1).astype(BF16)
            at = pl.multiple_of(place * HD, HD)
            mine[:, pl.ds(at, HD)] = both[:MOSTC]
            theirs[:, pl.ds(at, HD)] = both[MOSTC:]


def call(kernel, out_shape, n_smem, n_vmem, scratch=(), flops=1000000, data=1000000, far=()):
    many = isinstance(out_shape, tuple)
    return pl.pallas_call(
        kernel,
        out_shape=out_shape,
        in_specs=[
            pl.BlockSpec(memory_space=pltpu.HBM) if i in far else SMEM if i < n_smem else VMEM
            for i in range(n_smem + n_vmem)
        ],
        out_specs=tuple(VMEM for _ in out_shape) if many else VMEM,
        scratch_shapes=list(scratch),
        compiler_params=pltpu.CompilerParams(vmem_limit_bytes=24 * 1024 * 1024),
        cost_estimate=pl.CostEstimate(flops=flops, bytes_accessed=data, transcendentals=0),
    )


def on_device(
    tokens,
    norm_gain,
    q_weight,
    q_bias,
    kv_weight,
    kv_bias,
    out_weight,
    prefix_cache,
    span_lengths,
    prefix_lengths,
    slot_owner,
    head_order,
):
    core = lax.axis_index("core")
    y = lax.axis_index("y")
    x = lax.axis_index("x")
    zl = lax.axis_index("zl")
    j = y * 2 + core
    g = zl * 4 + x
    me = g * 8 + j
    span_len = span_lengths[0]
    slots = slot_owner[0]
    owner = lax.dynamic_index_in_dim(slots, me, 0, keepdims=False)
    other_owner = lax.dynamic_slice_in_dim(slots, me + 1 - 2 * core, 1, 0)
    sc = jnp.stack([core, y, j, owner, zl, x]).astype(jnp.int32)

    kinds = KVH * HD
    w_mine = lax.dynamic_slice_in_dim(kv_weight[0], core * kinds, kinds, 1)
    w_theirs = swap_core(lax.dynamic_slice_in_dim(kv_weight[0], (1 - core) * kinds, kinds, 1))
    bias = lax.dynamic_slice_in_dim(kv_bias, core * kinds + g * HD, HD, 1)
    blocks = call(cut_kernel, jax.ShapeDtypeStruct((8, ROWS, 3 * HD), BF16), 0, 3)(
        prefix_cache[0], w_mine, w_theirs
    )
    have = call(spread_kernel, jax.ShapeDtypeStruct((8, 2, D), BF16), 0, 1)(tokens[0])
    have = lax.all_to_all(have, ("zl", "x"), 0, 0, tiled=True)
    have, sc, blocks = lax.optimization_barrier((have, sc, blocks))
    blocks = lax.all_to_all(blocks, ("zl", "x"), 0, 0, tiled=True)

    have = have.reshape(16, D)
    own = [have] + [shift(have, "y", k) for k in range(1, 4)]
    gathered = own + [swap_core(one) for one in own]

    ow_theirs = swap_core(out_weight[0])

    piece = call(
        project_kernel, jax.ShapeDtypeStruct((2 * HD, SPAN), BF16), 1, 13,
        flops=2 * SPAN * D * 256, data=5 << 20,
    )(sc, norm_gain, q_weight[0], q_bias, bias, blocks, *gathered)
    pieces = [piece] + [shift(piece, "y", k) for k in range(1, 4)]
    mine, fresh = call(
        pack_kernel,
        (jax.ShapeDtypeStruct((5 * HD, SPAN), BF16), jax.ShapeDtypeStruct((HD, SPAN), BF16)),
        0, 4,
    )(*pieces)
    near = flip_x(fresh, 1)
    theirs = swap_core(mine)

    part = jax.ShapeDtypeStruct((4, HD + 16, SPAN), BF16)
    part_mine, part_theirs = call(
        attend_kernel, (part, part), 3, 3, flops=4 * 1024 * 2048 * 128, data=20 << 20
    )(sc, span_len, prefix_lengths[0], mine, theirs, blocks)

    part_theirs, near = lax.optimization_barrier((part_theirs, near))
    near = jnp.stack([fresh, near])
    two = flip_x(near, 2)
    swapped = swap_core(part_theirs)
    pairs = [jnp.stack([part_mine[k], swapped[k]]) for k in range(4)]
    pairs = [pairs[0]] + [shift(pairs[k], "y", -k) for k in range(1, 4)]
    pairs[3], two = lax.optimization_barrier((pairs[3], two))
    near = jnp.concatenate([near, two], axis=0)
    away = lax.ppermute(near, "zl", [(0, 1), (1, 0)])
    mixed = call(
        mix_kernel, jax.ShapeDtypeStruct((32, 2, D), BF16), 1, 6,
        flops=2 * 64 * 256 * D, data=6 << 20, far=(5, 6),
        scratch=(pltpu.VMEM((2 * HD, D), BF16), pltpu.SemaphoreType.DMA((16,))),
    )(sc, *pairs, out_weight[0], ow_theirs)
    mixed, away = lax.optimization_barrier((mixed, away))
    mixed = lax.all_to_all(mixed, ("zl", "x", "y"), 0, 0, tiled=True)
    half = jax.ShapeDtypeStruct((MOSTC, kinds), BF16)
    kept, sent = call(decode_kernel, (half, half), 4, 2)(
        sc, span_len, head_order[0], other_owner, near, away
    )
    got = swap_core(sent)
    mixed, got = lax.optimization_barrier((mixed, got))
    decode = jnp.where(
        core == 0, jnp.concatenate([kept, got], axis=1), jnp.concatenate([got, kept], axis=1)
    )
    total = jnp.sum(mixed.astype(F32), axis=0)
    handoff = shift((total + tokens[0].astype(F32)).astype(BF16), "section", 1)
    return (handoff[None], decode[None, None])


def solution(mesh):
    fine = Mesh(mesh.devices.reshape(4, 2, 4, 4, 2), tuple(SIZES))
    placed = (
        P("section", TP, None),
        P("section", None),
        P("section", None, TP),
        P("section", TP),
        P("section", TP, None),
        P("section", None),
        P("section", TP, None),
        P("section", TP, None),
        P("section", None),
        P("section", None),
        P("section", None),
        P("section", None),
    )
    return jax.shard_map(
        on_device,
        mesh=fine,
        in_specs=placed,
        out_specs=(P("section", TP, None), P("section", TP, None, None)),
        check_vma=False,
    )
```

```python
import jax
import jax.numpy as jnp
from jax import lax
from jax.experimental import pallas as pl
from jax.experimental.pallas import tpu as pltpu
from jax.sharding import Mesh, PartitionSpec as P

QH = 64
KVH = 8
HD = 128
D = 8192
SPAN = 128
REQS = 8
MOSTC = 32
ROWS = 256
EPS = 1e-06
NEG = -1e30
SCALE = HD ** (-0.5)
SIZES = {"section": 4, "zl": 2, "x": 4, "y": 4, "core": 2}
TP = ("zl", "x", "y", "core")
F32 = jnp.float32
BF16 = jnp.bfloat16
VMEM = pl.BlockSpec(memory_space=pltpu.VMEM)
SMEM = pl.BlockSpec(memory_space=pltpu.SMEM)


def dot(a, b, ca, cb):
    return lax.dot_general(a, b, (((ca,), (cb,)), ((), ())), preferred_element_type=F32)


def swap_core(block):
    return lax.ppermute(block, "core", [(0, 1), (1, 0)])


def flip_x(block, by):
    return lax.ppermute(block, "x", [(i, i ^ by) for i in range(4)])


def shift(block, axis, by):
    n = SIZES[axis]
    return lax.ppermute(block, axis, [(i, (i + by) % n) for i in range(n)])


def token_at(place):
    return ((place % 64) // 2) * 4 + (place // 64) * 2 + place % 2


def gathered_order(sc):
    row = lax.broadcasted_iota(jnp.int32, (SPAN, SPAN), 0)
    col = lax.broadcasted_iota(jnp.int32, (SPAN, SPAN), 1)
    core = jnp.where(row < 64, sc[0], 1 - sc[0])
    inner = row % 64
    y = (sc[1] - inner // 16 + 4) % 4
    place = core * 64 + (((inner % 16) // 2) * 4 + y) * 2 + inner % 2
    return jnp.where(place == col, 1.0, 0.0).astype(BF16)


def spread_kernel(tokens, out):
    one = tokens[...]
    for p in range(8):
        out[p] = one


def cut_kernel(cache, mine, theirs, out):
    for g in range(8):
        cols = slice(g * HD, (g + 1) * HD)
        out[g, :, 0:HD] = cache[:, cols]
        out[g, :, HD:2 * HD] = cache[:, (KVH + g) * HD:(KVH + g + 1) * HD]
        out[g, 0:HD, 2 * HD:] = mine[:, cols]
        out[g, HD:, 2 * HD:] = theirs[:, cols]


def fresh_kernel(sc, gain, blocks, *rest):
    tokens, out, scale = rest[:8], rest[8], rest[9]
    core, y = sc[0], sc[1]
    blk = 1024
    ss = jnp.zeros((SPAN, 1), F32)
    for i in range(D // blk):
        cols = slice(i * blk, (i + 1) * blk)
        x = jnp.concatenate([ref[:, cols] for ref in tokens], axis=0).astype(F32)
        ss = ss + jnp.sum(x * x, axis=1, keepdims=True)
    acc = jnp.zeros((SPAN, HD), F32)
    for g in range(8):
        parts = []
        for owner in (core, 1 - core):
            cols = pl.ds(pl.multiple_of(((g * 4 + y) * 2 + owner) * HD, HD), HD)
            x = jnp.concatenate([ref[:, cols] for ref in tokens], axis=0).astype(F32)
            parts.append((x * gain[:, cols].astype(F32)).astype(BF16))
        acc = acc + dot(jnp.concatenate(parts, axis=1), blocks[g, :, 2 * HD:], 1, 0)
    out[...] = acc
    scale[...] = jnp.broadcast_to(lax.rsqrt(ss * (1.0 / D) + EPS), (SPAN, HD))


def project_kernel(sc, gain, qw, qb, bias, fresh, scale, *rest):
    tokens, out = rest[:8], rest[8]
    blk = 1024
    acc = jnp.zeros((SPAN, HD), F32)
    for i in range(D // blk):
        cols = slice(i * blk, (i + 1) * blk)
        x = jnp.concatenate([ref[:, cols] for ref in tokens], axis=0).astype(F32)
        h = (x * gain[:, cols].astype(F32)).astype(BF16)
        acc = acc + dot(h, qw[cols, :], 1, 0)
    rs = scale[...]
    q = ((acc * rs + qb[...].astype(F32)) * SCALE).astype(BF16)
    kv = (fresh[...] * rs + jnp.where(sc[1] == 0, 1.0, 0.0) * bias[...].astype(F32)).astype(BF16)
    out[...] = dot(jnp.concatenate([q, kv], axis=1), gathered_order(sc), 0, 0).astype(BF16)


def pack_kernel(a, b, c, d, out, fresh):
    total = jnp.zeros((HD, SPAN), F32)
    for k, ref in enumerate((a, b, c, d)):
        out[k * HD:(k + 1) * HD, :] = ref[0:HD, :]
        total = total + ref[HD:, :].astype(F32)
    rows = total.astype(BF16)
    out[4 * HD:, :] = rows
    fresh[...] = rows


def attend_kernel(sc, span_len, prefix_len, mine, theirs, blocks, part_mine, part_theirs):
    core, j = sc[0], sc[2]
    packs = (mine, theirs)
    qt = jnp.concatenate([ref[k * HD:(k + 1) * HD, :] for ref in packs for k in range(4)], axis=1)
    fresh = [ref[4 * HD:, :].astype(F32) for ref in packs]
    keys = jnp.where(core == 0, fresh[0], fresh[1]).astype(BF16)
    values = jnp.where(core == 0, fresh[1], fresh[0]).astype(BF16)

    tok = token_at(lax.broadcasted_iota(jnp.int32, (1, SPAN), 1))
    key_tok = token_at(lax.broadcasted_iota(jnp.int32, (SPAN, 1), 0))
    q_seg = jnp.zeros((1, SPAN), jnp.int32)
    k_seg = jnp.zeros((SPAN, 1), jnp.int32)
    end = jnp.int32(0)
    for r in range(REQS):
        end = end + span_len[r]
        q_seg = q_seg + (tok >= end).astype(jnp.int32)
        k_seg = k_seg + (key_tok >= end).astype(jnp.int32)
    ends = []
    end = jnp.int32(0)
    for r in range(REQS):
        end = end + prefix_len[r]
        ends.append(end)

    def masked(s, allowed):
        parts = [jnp.where(allowed, s[:, u * SPAN:(u + 1) * SPAN], NEG) for u in range(KVH)]
        return jnp.concatenate(parts, axis=1)

    allowed = (k_seg == q_seg) & (key_tok <= tok) & (key_tok // 16 == j)
    s = masked(dot(keys, qt, 0, 0), allowed)
    m = jnp.max(s, axis=0, keepdims=True)
    p = jnp.exp(s - m)
    l = jnp.sum(p, axis=0, keepdims=True)
    o = dot(values, p.astype(BF16), 1, 0)

    for i in range(8):
        first = (i * 8 + j) * ROWS
        pos = first + lax.broadcasted_iota(jnp.int32, (ROWS, 1), 0)
        seg = jnp.zeros((ROWS, 1), jnp.int32)
        for r in range(REQS):
            seg = seg + (pos >= ends[r]).astype(jnp.int32)
        s = masked(dot(blocks[i, :, 0:HD], qt, 1, 0), seg == q_seg)
        m_new = jnp.maximum(m, jnp.max(s, axis=0, keepdims=True))
        p = jnp.exp(s - m_new)
        alpha = jnp.exp(m - m_new)
        l = l * alpha + jnp.sum(p, axis=0, keepdims=True)
        o = o * alpha + dot(blocks[i, :, HD:2 * HD], p.astype(BF16), 0, 0)
        m = m_new

    some = m > 0.5 * NEG
    o = o * jnp.where(some, 1.0 / l, 0.0)
    lse = jnp.where(some, m + jnp.log(l), NEG)
    first = core == 0

    def by_token_core(row, k):
        a, b = row[:, k * SPAN:(k + 1) * SPAN], row[:, (4 + k) * SPAN:(5 + k) * SPAN]
        a, b = jnp.where(first, a, b), jnp.where(first, b, a)
        low = jnp.concatenate([a[:, :64], b[:, :64]], axis=1)
        high = jnp.concatenate([a[:, 64:], b[:, 64:]], axis=1)
        return jnp.where(first, low, high), jnp.where(first, high, low)

    at_row = lax.broadcasted_iota(jnp.int32, (16, SPAN), 0)
    for k in range(4):
        for ref, value, one in zip((part_mine, part_theirs), by_token_core(o, k), by_token_core(lse, k)):
            hi = one.astype(BF16).astype(F32)
            mid = (one - hi).astype(BF16).astype(F32)
            stats = jnp.where(at_row == 0, hi, jnp.where(at_row == 1, mid, one - hi - mid))
            ref[k, 0:HD, :] = value.astype(BF16)
            ref[k, HD:HD + 16, :] = stats.astype(BF16)


def mix_kernel(sc, a, b, c, d, ow_mine, ow_theirs, out):
    blk = 1024
    pieces = [(ref, i) for ref in (a, b, c, d) for i in range(2)]
    lse = []
    for ref, i in pieces:
        stats = ref[i, HD:HD + 16, :].astype(F32)
        lse.append(stats[0:1, :] + stats[1:2, :] + stats[2:3, :])
    top = lse[0]
    for one in lse[1:]:
        top = jnp.maximum(top, one)
    total = jnp.zeros((1, SPAN), F32)
    acc = jnp.zeros((HD, SPAN), F32)
    for (ref, i), one in zip(pieces, lse):
        w = jnp.exp(one - top)
        total = total + w
        acc = acc + ref[i, 0:HD, :].astype(F32) * w
    att = jnp.transpose(acc / total)
    first = sc[0] == 0
    mine = jnp.where(first, att[:64], att[64:])
    theirs = jnp.where(first, att[64:], att[:64])
    mine, theirs = mine.astype(BF16), theirs.astype(BF16)
    for i in range(D // blk):
        cols = slice(i * blk, (i + 1) * blk)
        sums = dot(mine, ow_mine[:, cols], 1, 0) + dot(theirs, ow_theirs[:, cols], 1, 0)
        for p in range(32):
            out[p, :, cols] = sums[2 * p:2 * p + 2].astype(BF16)


def decode_kernel(sc, span_len, order, other_owner, near, away, mine, theirs):
    zl, x = sc[4], sc[5]
    row = lax.broadcasted_iota(jnp.int32, (MOSTC, SPAN), 0)
    col = lax.broadcasted_iota(jnp.int32, (MOSTC, SPAN), 1)
    picks = []
    for owner in (sc[3], other_owner[0]):
        start = jnp.int32(0)
        count = jnp.int32(0)
        for r in range(REQS):
            start = start + jnp.where(r < owner, span_len[r], 0)
            count = count + jnp.where(r == owner, span_len[r], 0)
        picks.append(jnp.where((row < count) & (token_at(col) == start + row), 1.0, 0.0).astype(BF16))
    pick = jnp.concatenate(picks, axis=0)
    for far, ref in enumerate((near, away)):
        for k in range(4):
            head = ((zl + far) % 2) * 4 + (x ^ k)
            place = jnp.int32(0)
            for p in range(KVH):
                place = place + jnp.where(order[p] == head, p, 0)
            both = dot(pick, ref[k], 1, 1).astype(BF16)
            at = pl.multiple_of(place * HD, HD)
            mine[:, pl.ds(at, HD)] = both[:MOSTC]
            theirs[:, pl.ds(at, HD)] = both[MOSTC:]


def call(kernel, out_shape, n_smem, n_vmem, scratch=(), flops=1000000, data=1000000, far=()):
    many = isinstance(out_shape, tuple)
    return pl.pallas_call(
        kernel,
        out_shape=out_shape,
        in_specs=[
            pl.BlockSpec(memory_space=pltpu.HBM) if i in far else SMEM if i < n_smem else VMEM
            for i in range(n_smem + n_vmem)
        ],
        out_specs=tuple(VMEM for _ in out_shape) if many else VMEM,
        scratch_shapes=list(scratch),
        compiler_params=pltpu.CompilerParams(vmem_limit_bytes=24 * 1024 * 1024),
        cost_estimate=pl.CostEstimate(flops=flops, bytes_accessed=data, transcendentals=0),
    )


def on_device(
    tokens,
    norm_gain,
    q_weight,
    q_bias,
    kv_weight,
    kv_bias,
    out_weight,
    prefix_cache,
    span_lengths,
    prefix_lengths,
    slot_owner,
    head_order,
):
    core = lax.axis_index("core")
    y = lax.axis_index("y")
    x = lax.axis_index("x")
    zl = lax.axis_index("zl")
    j = y * 2 + core
    g = zl * 4 + x
    me = g * 8 + j
    span_len = span_lengths[0]
    slots = slot_owner[0]
    owner = lax.dynamic_index_in_dim(slots, me, 0, keepdims=False)
    other_owner = lax.dynamic_slice_in_dim(slots, me + 1 - 2 * core, 1, 0)
    sc = jnp.stack([core, y, j, owner, zl, x]).astype(jnp.int32)

    kinds = KVH * HD
    w_mine = lax.dynamic_slice_in_dim(kv_weight[0], core * kinds, kinds, 1)
    w_theirs = swap_core(lax.dynamic_slice_in_dim(kv_weight[0], (1 - core) * kinds, kinds, 1))
    bias = lax.dynamic_slice_in_dim(kv_bias, core * kinds + g * HD, HD, 1)
    blocks = call(cut_kernel, jax.ShapeDtypeStruct((8, ROWS, 3 * HD), BF16), 0, 3)(
        prefix_cache[0], w_mine, w_theirs
    )
    have = call(spread_kernel, jax.ShapeDtypeStruct((8, 2, D), BF16), 0, 1)(tokens[0])
    have = lax.all_to_all(have, ("zl", "x"), 0, 0, tiled=True)
    have, sc, blocks = lax.optimization_barrier((have, sc, blocks))
    blocks = lax.all_to_all(blocks, ("zl", "x"), 0, 0, tiled=True)

    have = have.reshape(16, D)
    own = [have] + [shift(have, "y", k) for k in range(1, 4)]
    gathered = own + [swap_core(one) for one in own]

    ow_theirs = swap_core(out_weight[0])

    wide = jax.ShapeDtypeStruct((SPAN, HD), F32)
    share, scale = call(
        fresh_kernel, (wide, wide), 1, 10, flops=2 * SPAN * D * 256, data=4 << 20
    )(sc, norm_gain, blocks, *gathered)
    piece = call(
        project_kernel, jax.ShapeDtypeStruct((2 * HD, SPAN), BF16), 1, 14,
        flops=2 * SPAN * D * 256, data=5 << 20,
    )(sc, norm_gain, q_weight[0], q_bias, bias, share, scale, *gathered)
    pieces = [piece] + [shift(piece, "y", k) for k in range(1, 4)]
    mine, fresh = call(
        pack_kernel,
        (jax.ShapeDtypeStruct((5 * HD, SPAN), BF16), jax.ShapeDtypeStruct((HD, SPAN), BF16)),
        0, 4,
    )(*pieces)
    near = flip_x(fresh, 1)
    theirs = swap_core(mine)

    part = jax.ShapeDtypeStruct((4, HD + 16, SPAN), BF16)
    part_mine, part_theirs = call(
        attend_kernel, (part, part), 3, 3, flops=4 * 1024 * 2048 * 128, data=20 << 20
    )(sc, span_len, prefix_lengths[0], mine, theirs, blocks)

    part_theirs, near = lax.optimization_barrier((part_theirs, near))
    near = jnp.stack([fresh, near])
    two = flip_x(near, 2)
    swapped = swap_core(part_theirs)
    pairs = [jnp.stack([part_mine[k], swapped[k]]) for k in range(4)]
    pairs = [pairs[0]] + [shift(pairs[k], "y", -k) for k in range(1, 4)]
    pairs[3], two = lax.optimization_barrier((pairs[3], two))
    near = jnp.concatenate([near, two], axis=0)
    away = lax.ppermute(near, "zl", [(0, 1), (1, 0)])
    mixed = call(
        mix_kernel, jax.ShapeDtypeStruct((32, 2, D), BF16), 1, 6,
        flops=2 * 64 * 256 * D, data=6 << 20,
    )(sc, *pairs, out_weight[0], ow_theirs)
    mixed, away = lax.optimization_barrier((mixed, away))
    mixed = lax.all_to_all(mixed, ("zl", "x", "y"), 0, 0, tiled=True)
    half = jax.ShapeDtypeStruct((MOSTC, kinds), BF16)
    kept, sent = call(decode_kernel, (half, half), 4, 2)(
        sc, span_len, head_order[0], other_owner, near, away
    )
    got = swap_core(sent)
    mixed, got = lax.optimization_barrier((mixed, got))
    decode = jnp.where(
        core == 0, jnp.concatenate([kept, got], axis=1), jnp.concatenate([got, kept], axis=1)
    )
    total = jnp.sum(mixed.astype(F32), axis=0)
    handoff = shift((total + tokens[0].astype(F32)).astype(BF16), "section", 1)
    return (handoff[None], decode[None, None])


def solution(mesh):
    fine = Mesh(mesh.devices.reshape(4, 2, 4, 4, 2), tuple(SIZES))
    placed = (
        P("section", TP, None),
        P("section", None),
        P("section", None, TP),
        P("section", TP),
        P("section", TP, None),
        P("section", None),
        P("section", TP, None),
        P("section", TP, None),
        P("section", None),
        P("section", None),
        P("section", None),
        P("section", None),
    )
    return jax.shard_map(
        on_device,
        mesh=fine,
        in_specs=placed,
        out_specs=(P("section", TP, None), P("section", TP, None, None)),
        check_vma=False,
    )
```

```python
import jax
import jax.numpy as jnp
from jax import lax
from jax.experimental import pallas as pl
from jax.experimental.pallas import tpu as pltpu
from jax.sharding import Mesh, PartitionSpec as P

QH = 64
KVH = 8
HD = 128
D = 8192
SPAN = 128
REQS = 8
MOSTC = 32
ROWS = 256
EPS = 1e-06
NEG = -1e30
SCALE = HD ** (-0.5)
SIZES = {"section": 4, "zl": 2, "x": 4, "y": 4, "core": 2}
TP = ("zl", "x", "y", "core")
F32 = jnp.float32
BF16 = jnp.bfloat16
VMEM = pl.BlockSpec(memory_space=pltpu.VMEM)
SMEM = pl.BlockSpec(memory_space=pltpu.SMEM)


def dot(a, b, ca, cb):
    return lax.dot_general(a, b, (((ca,), (cb,)), ((), ())), preferred_element_type=F32)


def swap_core(block):
    return lax.ppermute(block, "core", [(0, 1), (1, 0)])


def flip_x(block, by):
    return lax.ppermute(block, "x", [(i, i ^ by) for i in range(4)])


def shift(block, axis, by):
    n = SIZES[axis]
    return lax.ppermute(block, axis, [(i, (i + by) % n) for i in range(n)])


def token_at(place):
    return ((place % 64) // 2) * 4 + (place // 64) * 2 + place % 2


def gathered_order(sc):
    row = lax.broadcasted_iota(jnp.int32, (SPAN, SPAN), 0)
    col = lax.broadcasted_iota(jnp.int32, (SPAN, SPAN), 1)
    core = jnp.where(row < 64, sc[0], 1 - sc[0])
    inner = row % 64
    y = (sc[1] - inner // 16 + 4) % 4
    place = core * 64 + (((inner % 16) // 2) * 4 + y) * 2 + inner % 2
    return jnp.where(place == col, 1.0, 0.0).astype(BF16)


def spread_kernel(tokens, out):
    one = tokens[...]
    for p in range(8):
        out[p] = one


def cut_kernel(cache, mine, theirs, out):
    for g in range(8):
        cols = slice(g * HD, (g + 1) * HD)
        out[g, :, 0:HD] = cache[:, cols]
        out[g, :, HD:2 * HD] = cache[:, (KVH + g) * HD:(KVH + g + 1) * HD]
        out[g, 0:HD, 2 * HD:] = mine[:, cols]
        out[g, HD:, 2 * HD:] = theirs[:, cols]


def fresh_kernel(sc, gain, blocks, *rest):
    tokens, out, scale = rest[:8], rest[8], rest[9]
    core, y = sc[0], sc[1]
    blk = 1024
    ss = jnp.zeros((SPAN, 1), F32)
    for i in range(D // blk):
        cols = slice(i * blk, (i + 1) * blk)
        x = jnp.concatenate([ref[:, cols] for ref in tokens], axis=0).astype(F32)
        ss = ss + jnp.sum(x * x, axis=1, keepdims=True)
    acc = jnp.zeros((SPAN, HD), F32)
    for g in range(8):
        parts = []
        for owner in (core, 1 - core):
            cols = pl.ds(pl.multiple_of(((g * 4 + y) * 2 + owner) * HD, HD), HD)
            x = jnp.concatenate([ref[:, cols] for ref in tokens], axis=0).astype(F32)
            parts.append((x * gain[:, cols].astype(F32)).astype(BF16))
        acc = acc + dot(jnp.concatenate(parts, axis=1), blocks[g, :, 2 * HD:], 1, 0)
    out[...] = acc
    scale[...] = jnp.broadcast_to(lax.rsqrt(ss * (1.0 / D) + EPS), (SPAN, HD))


def project_kernel(sc, gain, qw, qb, bias, fresh, scale, *rest):
    tokens, out = rest[:8], rest[8]
    blk = 1024
    acc = jnp.zeros((SPAN, HD), F32)
    for i in range(D // blk):
        cols = slice(i * blk, (i + 1) * blk)
        x = jnp.concatenate([ref[:, cols] for ref in tokens], axis=0).astype(F32)
        h = (x * gain[:, cols].astype(F32)).astype(BF16)
        acc = acc + dot(h, qw[cols, :], 1, 0)
    rs = scale[...]
    q = ((acc * rs + qb[...].astype(F32)) * SCALE).astype(BF16)
    kv = (fresh[...] * rs + jnp.where(sc[1] == 0, 1.0, 0.0) * bias[...].astype(F32)).astype(BF16)
    out[...] = dot(jnp.concatenate([q, kv], axis=1), gathered_order(sc), 0, 0).astype(BF16)


def summed(refs):
    total = refs[0][HD:, :].astype(F32)
    for ref in refs[1:]:
        total = total + ref[HD:, :].astype(F32)
    return total.astype(BF16)


def sum_kernel(a, b, c, d, fresh):
    fresh[...] = summed((a, b, c, d))


def attend_kernel(sc, span_len, prefix_len, blocks, *rest):
    core, j = sc[0], sc[2]
    mine, theirs, part_mine, part_theirs = rest[:4], rest[4:8], rest[8], rest[9]
    qt = jnp.concatenate([ref[0:HD, :] for ref in rest[:8]], axis=1)
    fresh = [summed(refs).astype(F32) for refs in (mine, theirs)]
    keys = jnp.where(core == 0, fresh[0], fresh[1]).astype(BF16)
    values = jnp.where(core == 0, fresh[1], fresh[0]).astype(BF16)

    tok = token_at(lax.broadcasted_iota(jnp.int32, (1, SPAN), 1))
    key_tok = token_at(lax.broadcasted_iota(jnp.int32, (SPAN, 1), 0))
    q_seg = jnp.zeros((1, SPAN), jnp.int32)
    k_seg = jnp.zeros((SPAN, 1), jnp.int32)
    end = jnp.int32(0)
    for r in range(REQS):
        end = end + span_len[r]
        q_seg = q_seg + (tok >= end).astype(jnp.int32)
        k_seg = k_seg + (key_tok >= end).astype(jnp.int32)
    ends = []
    end = jnp.int32(0)
    for r in range(REQS):
        end = end + prefix_len[r]
        ends.append(end)

    def masked(s, allowed):
        parts = [jnp.where(allowed, s[:, u * SPAN:(u + 1) * SPAN], NEG) for u in range(KVH)]
        return jnp.concatenate(parts, axis=1)

    allowed = (k_seg == q_seg) & (key_tok <= tok) & (key_tok // 16 == j)
    s = masked(dot(keys, qt, 0, 0), allowed)
    m = jnp.max(s, axis=0, keepdims=True)
    p = jnp.exp(s - m)
    l = jnp.sum(p, axis=0, keepdims=True)
    o = dot(values, p.astype(BF16), 1, 0)

    for i in range(8):
        first = (i * 8 + j) * ROWS
        pos = first + lax.broadcasted_iota(jnp.int32, (ROWS, 1), 0)
        seg = jnp.zeros((ROWS, 1), jnp.int32)
        for r in range(REQS):
            seg = seg + (pos >= ends[r]).astype(jnp.int32)
        s = masked(dot(blocks[i, :, 0:HD], qt, 1, 0), seg == q_seg)
        m_new = jnp.maximum(m, jnp.max(s, axis=0, keepdims=True))
        p = jnp.exp(s - m_new)
        alpha = jnp.exp(m - m_new)
        l = l * alpha + jnp.sum(p, axis=0, keepdims=True)
        o = o * alpha + dot(blocks[i, :, HD:2 * HD], p.astype(BF16), 0, 0)
        m = m_new

    some = m > 0.5 * NEG
    o = o * jnp.where(some, 1.0 / l, 0.0)
    lse = jnp.where(some, m + jnp.log(l), NEG)
    first = core == 0

    def by_token_core(row, k):
        a, b = row[:, k * SPAN:(k + 1) * SPAN], row[:, (4 + k) * SPAN:(5 + k) * SPAN]
        a, b = jnp.where(first, a, b), jnp.where(first, b, a)
        low = jnp.concatenate([a[:, :64], b[:, :64]], axis=1)
        high = jnp.concatenate([a[:, 64:], b[:, 64:]], axis=1)
        return jnp.where(first, low, high), jnp.where(first, high, low)

    at_row = lax.broadcasted_iota(jnp.int32, (16, SPAN), 0)
    for k in range(4):
        for ref, value, one in zip((part_mine, part_theirs), by_token_core(o, k), by_token_core(lse, k)):
            hi = one.astype(BF16).astype(F32)
            mid = (one - hi).astype(BF16).astype(F32)
            stats = jnp.where(at_row == 0, hi, jnp.where(at_row == 1, mid, one - hi - mid))
            ref[k, 0:HD, :] = value.astype(BF16)
            ref[k, HD:HD + 16, :] = stats.astype(BF16)


def mix_kernel(sc, a, b, c, d, ow_mine, ow_theirs, out):
    blk = 1024
    pieces = [(ref, i) for ref in (a, b, c, d) for i in range(2)]
    lse = []
    for ref, i in pieces:
        stats = ref[i, HD:HD + 16, :].astype(F32)
        lse.append(stats[0:1, :] + stats[1:2, :] + stats[2:3, :])
    top = lse[0]
    for one in lse[1:]:
        top = jnp.maximum(top, one)
    total = jnp.zeros((1, SPAN), F32)
    acc = jnp.zeros((HD, SPAN), F32)
    for (ref, i), one in zip(pieces, lse):
        w = jnp.exp(one - top)
        total = total + w
        acc = acc + ref[i, 0:HD, :].astype(F32) * w
    att = jnp.transpose(acc / total)
    first = sc[0] == 0
    mine = jnp.where(first, att[:64], att[64:])
    theirs = jnp.where(first, att[64:], att[:64])
    mine, theirs = mine.astype(BF16), theirs.astype(BF16)
    for i in range(D // blk):
        cols = slice(i * blk, (i + 1) * blk)
        sums = dot(mine, ow_mine[:, cols], 1, 0) + dot(theirs, ow_theirs[:, cols], 1, 0)
        for p in range(32):
            out[p, :, cols] = sums[2 * p:2 * p + 2].astype(BF16)


def decode_kernel(sc, span_len, order, other_owner, near, away, mine, theirs):
    zl, x = sc[4], sc[5]
    row = lax.broadcasted_iota(jnp.int32, (MOSTC, SPAN), 0)
    col = lax.broadcasted_iota(jnp.int32, (MOSTC, SPAN), 1)
    picks = []
    for owner in (sc[3], other_owner[0]):
        start = jnp.int32(0)
        count = jnp.int32(0)
        for r in range(REQS):
            start = start + jnp.where(r < owner, span_len[r], 0)
            count = count + jnp.where(r == owner, span_len[r], 0)
        picks.append(jnp.where((row < count) & (token_at(col) == start + row), 1.0, 0.0).astype(BF16))
    pick = jnp.concatenate(picks, axis=0)
    for far, ref in enumerate((near, away)):
        for k in range(4):
            head = ((zl + far) % 2) * 4 + (x ^ k)
            place = jnp.int32(0)
            for p in range(KVH):
                place = place + jnp.where(order[p] == head, p, 0)
            both = dot(pick, ref[k], 1, 1).astype(BF16)
            at = pl.multiple_of(place * HD, HD)
            mine[:, pl.ds(at, HD)] = both[:MOSTC]
            theirs[:, pl.ds(at, HD)] = both[MOSTC:]


def call(kernel, out_shape, n_smem, n_vmem, scratch=(), flops=1000000, data=1000000, far=()):
    many = isinstance(out_shape, tuple)
    return pl.pallas_call(
        kernel,
        out_shape=out_shape,
        in_specs=[
            pl.BlockSpec(memory_space=pltpu.HBM) if i in far else SMEM if i < n_smem else VMEM
            for i in range(n_smem + n_vmem)
        ],
        out_specs=tuple(VMEM for _ in out_shape) if many else VMEM,
        scratch_shapes=list(scratch),
        compiler_params=pltpu.CompilerParams(vmem_limit_bytes=24 * 1024 * 1024),
        cost_estimate=pl.CostEstimate(flops=flops, bytes_accessed=data, transcendentals=0),
    )


def on_device(
    tokens,
    norm_gain,
    q_weight,
    q_bias,
    kv_weight,
    kv_bias,
    out_weight,
    prefix_cache,
    span_lengths,
    prefix_lengths,
    slot_owner,
    head_order,
):
    core = lax.axis_index("core")
    y = lax.axis_index("y")
    x = lax.axis_index("x")
    zl = lax.axis_index("zl")
    j = y * 2 + core
    g = zl * 4 + x
    me = g * 8 + j
    span_len = span_lengths[0]
    slots = slot_owner[0]
    owner = lax.dynamic_index_in_dim(slots, me, 0, keepdims=False)
    other_owner = lax.dynamic_slice_in_dim(slots, me + 1 - 2 * core, 1, 0)
    sc = jnp.stack([core, y, j, owner, zl, x]).astype(jnp.int32)

    kinds = KVH * HD
    w_mine = lax.dynamic_slice_in_dim(kv_weight[0], core * kinds, kinds, 1)
    w_theirs = swap_core(lax.dynamic_slice_in_dim(kv_weight[0], (1 - core) * kinds, kinds, 1))
    bias = lax.dynamic_slice_in_dim(kv_bias, core * kinds + g * HD, HD, 1)
    blocks = call(cut_kernel, jax.ShapeDtypeStruct((8, ROWS, 3 * HD), BF16), 0, 3)(
        prefix_cache[0], w_mine, w_theirs
    )
    have = call(spread_kernel, jax.ShapeDtypeStruct((8, 2, D), BF16), 0, 1)(tokens[0])
    have = lax.all_to_all(have, ("zl", "x"), 0, 0, tiled=True)
    have, sc, blocks = lax.optimization_barrier((have, sc, blocks))
    blocks = lax.all_to_all(blocks, ("zl", "x"), 0, 0, tiled=True)

    have = have.reshape(16, D)
    own = [have] + [shift(have, "y", k) for k in range(1, 4)]
    gathered = own + [swap_core(one) for one in own]

    ow_theirs = swap_core(out_weight[0])

    wide = jax.ShapeDtypeStruct((SPAN, HD), F32)
    share, scale = call(
        fresh_kernel, (wide, wide), 1, 10, flops=2 * SPAN * D * 256, data=4 << 20
    )(sc, norm_gain, blocks, *gathered)
    piece = call(
        project_kernel, jax.ShapeDtypeStruct((2 * HD, SPAN), BF16), 1, 14,
        flops=2 * SPAN * D * 256, data=5 << 20,
    )(sc, norm_gain, q_weight[0], q_bias, bias, share, scale, *gathered)
    pieces = [piece] + [shift(piece, "y", k) for k in range(1, 4)]
    crossed = [swap_core(one) for one in pieces]
    fresh = call(sum_kernel, jax.ShapeDtypeStruct((HD, SPAN), BF16), 0, 4)(*pieces)
    near = flip_x(fresh, 1)

    part = jax.ShapeDtypeStruct((4, HD + 16, SPAN), BF16)
    part_mine, part_theirs = call(
        attend_kernel, (part, part), 3, 9, flops=4 * 1024 * 2048 * 128, data=20 << 20
    )(sc, span_len, prefix_lengths[0], blocks, *pieces, *crossed)

    part_theirs, near = lax.optimization_barrier((part_theirs, near))
    near = jnp.stack([fresh, near])
    two = flip_x(near, 2)
    swapped = swap_core(part_theirs)
    pairs = [jnp.stack([part_mine[k], swapped[k]]) for k in range(4)]
    pairs = [pairs[0]] + [shift(pairs[k], "y", -k) for k in range(1, 4)]
    pairs[3], two = lax.optimization_barrier((pairs[3], two))
    near = jnp.concatenate([near, two], axis=0)
    away = lax.ppermute(near, "zl", [(0, 1), (1, 0)])
    mixed = call(
        mix_kernel, jax.ShapeDtypeStruct((32, 2, D), BF16), 1, 6,
        flops=2 * 64 * 256 * D, data=6 << 20,
    )(sc, *pairs, out_weight[0], ow_theirs)
    mixed, away = lax.optimization_barrier((mixed, away))
    mixed = lax.all_to_all(mixed, ("zl", "x", "y"), 0, 0, tiled=True)
    half = jax.ShapeDtypeStruct((MOSTC, kinds), BF16)
    kept, sent = call(decode_kernel, (half, half), 4, 2)(
        sc, span_len, head_order[0], other_owner, near, away
    )
    got = swap_core(sent)
    mixed, got = lax.optimization_barrier((mixed, got))
    decode = jnp.where(
        core == 0, jnp.concatenate([kept, got], axis=1), jnp.concatenate([got, kept], axis=1)
    )
    total = jnp.sum(mixed.astype(F32), axis=0)
    handoff = shift((total + tokens[0].astype(F32)).astype(BF16), "section", 1)
    return (handoff[None], decode[None, None])


def solution(mesh):
    fine = Mesh(mesh.devices.reshape(4, 2, 4, 4, 2), tuple(SIZES))
    placed = (
        P("section", TP, None),
        P("section", None),
        P("section", None, TP),
        P("section", TP),
        P("section", TP, None),
        P("section", None),
        P("section", TP, None),
        P("section", TP, None),
        P("section", None),
        P("section", None),
        P("section", None),
        P("section", None),
    )
    return jax.shard_map(
        on_device,
        mesh=fine,
        in_specs=placed,
        out_specs=(P("section", TP, None), P("section", TP, None, None)),
        check_vma=False,
    )
```
